512 devices in a mesh: wide: 128 (over z, y, core), narrow: 4 (over x).
Axes of the slice: x: 4, y: 4, z: 16, core: 2. Of those that a mesh axis runs over, the one named last changes fastest.
Arguments:
- coefficients: bfloat16 [100, 2097152], P(None, ('wide', 'narrow')), may hold values from -6 to 6
- neighbours: int32 [4, 2097152], P(None, ('wide', 'narrow')), may hold values from 0 to 5119, as said below
- halo_blocks: int32 [512, 4, 2], P(('wide', 'narrow')), may hold values from 0 to 31, as said below
- recon_weight: bfloat16 [5, 75, 100], replicated, may hold values from -0.25 to 0.25
- owner_device: int32 [16384], P(('wide', 'narrow')), may hold values from 0 to 511, as said below
- work_count: int32 [16384], P(('wide', 'narrow')), may hold values from 1 to 4
Outputs:
- migrated_modal: bfloat16 [100, 2097152], P(None, ('wide', 'narrow'))
- migrated_metric: float32 [6, 2097152], P(None, ('wide', 'narrow'))
- migrated_work: float32 [2097152], P(('wide', 'narrow'))
The draws below stay inside these ranges and needn't reach their ends.
Inputs may be any that keep to these rules, and one draw needn't show every extreme that they name: `neighbours`: A value below 4096 names an element of the same device; a larger one names element i of the h-th block sent to this device from direction k, as in the reference program. `halo_blocks`: each device's list for one direction holds 2 different block numbers of that device. `owner_device`: every device receives exactly 32 blocks. Of one device's blocks, either exactly 1 or none go to devices of any one wide index. Two devices of the same wide index with narrow indices 2j and 2j + 1 together send either exactly 1 or none of their blocks to devices of any one wide index. For every wide index w and narrow indices a and c, exactly 8 of the blocks that devices of narrow index a send to wide index w go to the device of wide index w and narrow index c.
All inputs are finite; a program needn't handle non-finite values.
Results may differ from the reference program's by a relative error of at most 0.0004.
Values may be sent and summed in bfloat16 or wider, within the bound.
A program may use at most 64 MiB of HBM per device.

```python
from functools import partial
import jax
import jax.numpy as jnp
from jax import lax

BLK = 128
BLOCKS_DEV = 32
COEF = 100
DERIV = 75
HALO_BLOCKS = 2
ELEMS = 2097152
BLOCKS = 16384
N_WIDE = 128
N_NARROW = 4
DEVICES = 512


def draw_neighbours(key, part):
    base = jax.random.fold_in(key, 17)
    elems_dev = BLOCKS_DEV * BLK
    halo_size = 4 * HALO_BLOCKS * BLK
    shape_all = (4, DEVICES * elems_dev)
    near = jax.random.randint(jax.random.fold_in(base, 1), shape_all, 0, elems_dev)
    far_ref = jax.random.randint(jax.random.fold_in(base, 2), shape_all, 0, halo_size) + elems_dev
    choose_far = jax.random.randint(jax.random.fold_in(base, 3), shape_all, 0, 5) < 2
    return jnp.where(choose_far, far_ref, near).astype(jnp.int32)


def draw_halo_blocks(key, part):
    base = jax.random.fold_in(key, 23)
    subkeys = jax.random.split(base, DEVICES * 4)
    shuffles = jax.vmap(partial(jax.random.permutation, x=BLOCKS_DEV))(subkeys)
    return shuffles[:, :HALO_BLOCKS].reshape(DEVICES, 4, HALO_BLOCKS).astype(jnp.int32)


def draw_owner_device(key, part):
    base = jax.random.fold_in(key, 31)
    pair_count = N_NARROW // 2
    wide_perm = jax.vmap(partial(jax.random.permutation, x=N_WIDE))(jax.random.split(jax.random.fold_in(base, 1), pair_count))
    wide_start = jax.vmap(partial(jax.random.permutation, x=N_WIDE))(jax.random.split(jax.random.fold_in(base, 2), pair_count))
    labels = jax.vmap(partial(jax.random.permutation, x=BLOCKS_DEV))(jax.random.split(jax.random.fold_in(base, 3), N_WIDE * N_NARROW)) % N_NARROW
    labels = labels.reshape(N_WIDE, N_NARROW, BLOCKS_DEV)
    source_wide = jnp.arange(N_WIDE)[:, None, None]
    source_narrow = jnp.arange(N_NARROW)[None, :, None]
    pair_of = source_narrow // 2
    member = source_narrow % 2
    position = jnp.arange(BLOCKS_DEV)[None, None, :]
    target_wide = wide_perm[pair_of, (wide_start[pair_of, source_wide] + member * BLOCKS_DEV + position) % N_WIDE]
    target_narrow = labels[target_wide, source_narrow, position]
    return (target_wide * N_NARROW + target_narrow).reshape(-1).astype(jnp.int32)


def place_ends(values, key, smallest, largest):
    place = [jax.random.randint(jax.random.fold_in(key, axis), (), 0, length) for axis, length in enumerate(values.shape)]
    main_axis = values.shape.index(max(values.shape))
    next_to = place[:main_axis] + [(place[main_axis] + 1) % values.shape[main_axis]] + place[main_axis + 1:]
    return values.at[tuple(place)].set(smallest).at[tuple(next_to)].set(largest)


def block_levels(stream_key, dims, cuts, low, largest):
    def one(dim, blocks):
        heights = jax.random.uniform(jax.random.fold_in(jax.random.fold_in(stream_key, 6), dim), (blocks,), jnp.float32, low / len(cuts), largest / len(cuts))
        return jnp.repeat(jnp.exp(heights), dims[dim] // blocks).reshape((-1,) + (1,) * (len(dims) - dim - 1))

    loudness = one(*cuts[0])
    for cut in cuts[1:]:
        loudness = loudness * one(*cut)
    return loudness


def bell_draw(own_key, extent, spread, bound, cuts=(), kind=jnp.bfloat16):
    drawn = jax.random.normal(own_key, extent, jnp.float32) * spread
    if len(cuts) > 0:
        drawn = block_levels(own_key, extent, cuts, -0.22, 0.18) * drawn
    return jnp.clip(drawn, min=-bound, max=bound).astype(kind)


def setup_inputs(seed: int = 0) -> dict:
    key_list = jax.random.split(jax.random.key(seed), 7)
    coefficients = bell_draw(key_list[0], (COEF, ELEMS), 1.0, 6.0, ((1, 512),))
    neighbours = draw_neighbours(jax.random.fold_in(key_list[6], 71), 0)
    halo_blocks = draw_halo_blocks(jax.random.fold_in(key_list[6], 71), 0)
    recon_weight = bell_draw(key_list[3], (5, DERIV, COEF), (5 * COEF) ** -0.5, 0.25)
    owner_device = draw_owner_device(jax.random.fold_in(key_list[6], 71), 0)
    work_count = place_ends(jax.random.randint(key_list[5], (BLOCKS,), 1, 5), jax.random.fold_in(key_list[5], 1), 1, 4).astype(jnp.int32)
    return {"coefficients": coefficients, "neighbours": neighbours, "halo_blocks": halo_blocks, "recon_weight": recon_weight, "owner_device": owner_device, "work_count": work_count}


def metric_rows(derivs):
    vectors = derivs.reshape(derivs.shape[0] // 3, 3, derivs.shape[1])
    inverse = 1.0 / vectors.shape[0]
    along_x = vectors[:, 0]
    along_y = vectors[:, 1]
    along_z = vectors[:, 2]
    return jnp.stack([1.0 + inverse * lax.optimization_barrier(jnp.sum(along_x * along_x, axis=0)), 1.0 + inverse * lax.optimization_barrier(jnp.sum(along_y * along_y, axis=0)), 1.0 + inverse * lax.optimization_barrier(jnp.sum(along_z * along_z, axis=0)), inverse * lax.optimization_barrier(jnp.sum(along_x * along_y, axis=0)), inverse * lax.optimization_barrier(jnp.sum(along_x * along_z, axis=0)), inverse * lax.optimization_barrier(jnp.sum(along_y * along_z, axis=0))])

def determinant(components):
    metric_xx = components[0]
    metric_yy = components[1]
    metric_zz = components[2]
    metric_xy = components[3]
    metric_xz = components[4]
    metric_yz = components[5]
    return metric_xx * (metric_yy * metric_zz - metric_yz * metric_yz) - metric_xy * (metric_xy * metric_zz - metric_yz * metric_xz) + metric_xz * (metric_xy * metric_yz - metric_yy * metric_xz)

def reference(coefficients, neighbours, halo_blocks, recon_weight, owner_device, work_count):
    elems_dev = BLOCKS_DEV * BLK
    opposite = jnp.array([1, 0, 3, 2], dtype=jnp.int32)

    def one_device(device):
        wide_at = device // N_NARROW
        narrow_at = device % N_NARROW
        peer_ids = jnp.stack([(wide_at - 1) % N_WIDE * N_NARROW + narrow_at, (wide_at + 1) % N_WIDE * N_NARROW + narrow_at, wide_at * N_NARROW + (narrow_at - 1) % N_NARROW, wide_at * N_NARROW + (narrow_at + 1) % N_NARROW]).astype(jnp.int32)
        first_elem = (device * elems_dev).astype(jnp.int32)
        face_refs = lax.dynamic_slice_in_dim(neighbours, first_elem, elems_dev, 1)
        is_local = face_refs < elems_dev
        offset = jnp.maximum(face_refs - elems_dev, 0)
        slot_index = offset // BLK
        lane_index = offset % BLK
        direction = slot_index // HALO_BLOCKS
        listed = slot_index % HALO_BLOCKS
        sender = peer_ids[direction]
        block_index = halo_blocks[sender, opposite[direction], listed]
        source = jnp.where(is_local, first_elem + face_refs, sender * elems_dev + block_index * BLK + lane_index)
        own_cols = lax.dynamic_slice_in_dim(coefficients, first_elem, elems_dev, 1)
        derivs = jnp.dot(recon_weight[0], own_cols, preferred_element_type=jnp.float32)
        for face_index in range(4):
            gathered = jnp.take(coefficients, source[face_index], axis=1)
            derivs = derivs + jnp.dot(recon_weight[face_index + 1], gathered, preferred_element_type=jnp.float32)
        components = metric_rows(derivs)
        counts = lax.dynamic_slice_in_dim(work_count, (device * BLOCKS_DEV).astype(jnp.int32), BLOCKS_DEV, 0)
        work_est = jnp.repeat(counts.astype(jnp.float32), BLK) * jnp.sqrt(determinant(components))
        return (components, work_est)
    components, work_est = lax.map(one_device, jnp.arange(DEVICES, dtype=jnp.int32))
    metric_all = jnp.transpose(components, (1, 0, 2)).reshape(6, -1)
    work_all = work_est.reshape(-1)
    block_ids = jnp.arange(BLOCKS_DEV * DEVICES, dtype=jnp.int32)
    source_dev = block_ids // BLOCKS_DEV
    sort_key = owner_device * (BLOCKS_DEV * DEVICES) + (source_dev % N_NARROW * N_WIDE + source_dev // N_NARROW) * BLOCKS_DEV + block_ids % BLOCKS_DEV
    ordering = jnp.argsort(sort_key).astype(jnp.int32)

    def regroup(values):
        blocked = values.reshape(values.shape[0], -1, BLK)
        return jnp.take(blocked, ordering, axis=1).reshape(values.shape[0], -1)
    return (regroup(coefficients), regroup(metric_all), regroup(work_all[None, :])[0])
```

```python
import jax
import jax.numpy as jnp
from jax import lax
from jax.experimental import pallas as pl
from jax.experimental.pallas import tpu as pltpu
from jax.sharding import PartitionSpec as P

MESH = pl.DeviceIdType.MESH
WIDE = 128
NARROW = 4
BLK = 128
BLOCKS = 32
ELEMS = BLK * BLOCKS
COEF = 100
HALO = 8 * BLK
EXT = ELEMS + HALO
HALF = 16 * BLK
CODE = 1024

INFO, SWAP_A, SWAP_B, SWAP_C, HALO_UP, HALO_DOWN, HALO_LEFT, HALO_RIGHT = range(8)
WIDE_TAG, WIDE_A, WIDE_B, SWAP_L, WIDE_L, NARROW_C, NARROW_A, NARROW_B, NARROW_L = range(8, 17)
GROUPS = 17


def aligned(value, step):
    return pl.multiple_of(value, step)


def kernel(
    coef, nbr, halo, wts, info, modal, metric, work,
    tiles, pair_a, pair_b, pair_c, late, pinfo, both, pick_v, pick_s, tab_v, tab_s, cnt_v, cnt_r, cnt_s,
    hsend, hrecv, tags, tags2, send_a, recv_a, send_b, recv_b, send_l, recv_l,
    out_a, out_b, out_l, last, table, own, rows, sent, came, local,
):
    w = lax.axis_index("wide")
    a = lax.axis_index("narrow")
    h = lax.rem(a, 2)
    j = a // 2
    partner = a + 1 - 2 * h
    mine = pl.ds(h * BLOCKS, BLOCKS)
    pairs = (pair_a, pair_b, pair_c)

    def remote(src, dst, group, wide, narrow):
        return pltpu.make_async_remote_copy(
            src_ref=src, dst_ref=dst, send_sem=sent.at[group], recv_sem=came.at[group],
            device_id=(wide, narrow), device_id_type=MESH,
        )

    def wait_bytes(ref, sem):
        pltpu.make_async_copy(ref, ref, sem).wait()

    barrier = pltpu.get_barrier_semaphore()

    def greet(i, carry):
        pl.semaphore_signal(barrier, inc=1, device_id=(lax.rem(w + i, WIDE), a), device_id_type=MESH)
        return carry

    for d in range(1, NARROW):
        pl.semaphore_signal(barrier, inc=1, device_id=(w, lax.rem(a + d, NARROW)), device_id_type=MESH)
    lax.fori_loop(1, WIDE, greet, 0)
    pl.semaphore_wait(barrier, WIDE - 1 + NARROW - 1)

    swap_info = remote(info, pinfo, INFO, w, partner)
    swap_info.start()

    def retile(b, carry):
        at = pl.ds(aligned(b * BLK, BLK), BLK)
        for k in range(6):
            tiles[k, b] = coef[16 * k : 16 * k + 16, at]
        end = coef[96:100, at]
        tiles[6, b] = jnp.concatenate([end, jnp.zeros((12, BLK), end.dtype)], axis=0)
        return carry

    lax.fori_loop(0, BLOCKS, retile, 0)
    swaps = []
    for k in range(3):
        swap = remote(tiles.at[3 * (1 - h) + k], pairs[k].at[mine], SWAP_A + k, w, partner)
        swap.start()
        swaps.append(swap)

    places = [
        (lax.rem(w + WIDE - 1, WIDE), a),
        (lax.rem(w + 1, WIDE), a),
        (w, lax.rem(a + NARROW - 1, NARROW)),
        (w, lax.rem(a + 1, NARROW)),
    ]
    halos = []
    for k in range(4):
        for s in range(2):
            block = halo[k * 2 + s]
            for r in range(7):
                hsend[k, s, r] = tiles[r, block]
        push = remote(hsend.at[k], hrecv.at[k ^ 1], HALO_UP + k, *places[k])
        push.start()
        halos.append(push)

    def keep(b, carry):
        for k in range(3):
            pairs[k][h * BLOCKS + b] = tiles[3 * h + k, b]
        return carry

    lax.fori_loop(0, BLOCKS, keep, 0)

    swap_info.wait()
    both[...] = info[...] + pinfo[...]
    entries = jnp.transpose(jnp.broadcast_to(both[...], (BLK, BLK)))
    lane = lax.broadcasted_iota(jnp.int32, (BLK, BLK), 1)
    sub = lax.broadcasted_iota(jnp.int32, (BLK, BLK), 0)
    goes = (entries >= CODE) & ((entries & (CODE - 1)) // NARROW == lane)
    pick = jnp.sum(jnp.where(goes, sub, 0), axis=0, keepdims=True)
    pick_v[...] = jnp.broadcast_to(pick, (8, BLK))
    to_scalar = pltpu.make_async_copy(pick_v, pick_s, local.at[0])
    to_scalar.start()
    to_scalar.wait()

    def spread(src, dst, group):
        def one(i, carry):
            t = lax.rem(w + i, WIDE)
            remote(src.at[t], dst.at[w], group, t, a).start()
            return carry

        lax.fori_loop(1, WIDE, one, 0)

    swaps[0].wait()

    def pack_a(t, carry):
        send_a[t] = pair_a[pick_s[0, t]]
        return carry

    lax.fori_loop(0, WIDE, pack_a, 0)
    recv_a[w] = send_a[w]
    spread(send_a, recv_a, WIDE_A)

    swaps[1].wait()
    swaps[2].wait()

    def pack_b(t, carry):
        send_b[t, 0:16] = pair_b[pick_s[0, t]]
        send_b[t, 16:32] = pair_c[pick_s[0, t]]
        return carry

    lax.fori_loop(0, WIDE, pack_b, 0)
    recv_b[w] = send_b[w]
    spread(send_b, recv_b, WIDE_B)

    def one_tag(i, carry):
        remote(both, tags.at[w], WIDE_TAG, lax.rem(w + i, WIDE), a).start()
        return carry

    tags[w] = both[...]
    lax.fori_loop(1, WIDE, one_tag, 0)

    def product(cols, weights):
        return lax.dot_general(
            cols, weights, (((0,), (0,)), ((), ())), preferred_element_type=jnp.float32
        )

    def own_block(b, carry):
        at = pl.ds(aligned(b * BLK, BLK), BLK)
        result = product(coef[:, at], wts[...])
        own[at, :] = result[:, :BLK]
        for f in range(4):
            table[f, at, :] = result[:, (f + 1) * BLK : (f + 2) * BLK]
        return carry

    lax.fori_loop(0, BLOCKS, own_block, 0)
    for push in halos:
        push.wait()
    for k in range(4):
        for s in range(2):
            result = product(hrecv[k, s].reshape(112, BLK)[:COEF], wts[:, BLK:])
            first = ELEMS + (2 * k + s) * BLK
            for f in range(4):
                table[f, first : first + BLK, :] = result[:, f * BLK : (f + 1) * BLK]

    def gather(i, carry):
        for u in range(8):
            e = i * 8 + u
            total = table[0, nbr[0, e]]
            for f in range(1, 4):
                total = total + table[f, nbr[f, e]]
            rows[e] = total
        return carry

    lax.fori_loop(0, ELEMS // 8, gather, 0)

    def metric_block(b, carry):
        at = pl.ds(aligned(b * BLK, BLK), BLK)
        derivs = jnp.transpose(own[at, :] + rows[at, :])
        x, y, z = derivs[0:32], derivs[32:64], derivs[64:96]

        def mean(left, right, base):
            return base + jnp.sum(left * right, axis=0, keepdims=True) * (1.0 / 25)

        full = jnp.concatenate(
            [mean(x, x, 1.0), mean(y, y, 1.0), mean(z, z, 1.0), mean(x, y, 0.0), mean(x, z, 0.0), mean(y, z, 0.0)],
            axis=0,
        )
        high = full.astype(jnp.bfloat16).astype(jnp.float32)
        tail = coef[96:100, at].astype(jnp.float32)
        tile = jnp.concatenate([high, tail[0:2], full - high, tail[2:4]], axis=0)
        late[h * BLOCKS + b] = tile.astype(jnp.bfloat16)
        return carry

    lax.fori_loop(0, BLOCKS, metric_block, 0)

    swap_late = remote(late.at[mine], late.at[mine], SWAP_L, w, partner)
    swap_late.start()
    swap_late.wait()
    odd = lax.rem(w + h, 2)

    def pack_l(i, carry):
        t = 2 * i + h
        send_l[t] = late[pick_s[0, t]]
        return carry

    lax.fori_loop(0, WIDE // 2, pack_l, 0)

    def send_late(i, carry):
        t = lax.rem(w + 2 * i + odd, WIDE)
        remote(send_l.at[t], recv_l.at[w], WIDE_L, t, a).start()
        return carry

    @pl.when(odd == 0)
    def _():
        recv_l[w] = send_l[w]

    lax.fori_loop(1 - odd, WIDE // 2, send_late, 0)

    wait_bytes(tags.at[pl.ds(0, WIDE - 1)], came.at[WIDE_TAG])

    def flat(i, carry):
        tags2[pl.ds(i, 1), :] = tags[i]
        return carry

    lax.fori_loop(0, WIDE, flat, 0)
    codes = jnp.transpose(tags2[...])
    here = (codes >= CODE) & ((codes & (CODE - 1)) // NARROW == w)
    kinds = jnp.where(here, (sub // BLOCKS) * NARROW + lax.rem(codes, NARROW) + 1, 0)
    kind = jnp.sum(kinds, axis=0, keepdims=True) - 1
    count = jnp.sum(jnp.where(here, codes // CODE, 0), axis=0, keepdims=True)
    lane8 = lax.broadcasted_iota(jnp.int32, (8, BLK), 1)
    sub8 = lax.broadcasted_iota(jnp.int32, (8, BLK), 0)
    chosen = (jnp.broadcast_to(kind, (8, BLK)) == sub8).astype(jnp.int32)
    rank = chosen
    for step in (1, 2, 4, 8, 16, 32, 64):
        rank = rank + jnp.where(lane8 >= step, pltpu.roll(rank, step, 1), 0)
    rank = rank - chosen
    counts = jnp.broadcast_to(count, (8, BLK))
    froms = jnp.zeros((8, BLK), jnp.int32)
    works = jnp.zeros((8, BLK), jnp.int32)
    for r in range(8):
        found = (chosen > 0) & (rank == r)
        froms = jnp.where(
            lane8 == r, jnp.sum(jnp.where(found, lane8, 0), axis=1, keepdims=True), froms
        )
        works = jnp.where(
            lane8 == r, jnp.sum(jnp.where(found, counts, 0), axis=1, keepdims=True), works
        )
    tab_v[...] = froms
    cnt_v[...] = works
    to_scalar = pltpu.make_async_copy(tab_v, tab_s, local.at[1])
    to_scalar.start()
    to_scalar.wait()
    cnt_r[a] = cnt_v[...]
    for d in range(1, NARROW):
        remote(cnt_v, cnt_r.at[a], NARROW_C, w, lax.rem(a + d, NARROW)).start()

    def collect(src, dst):
        def one(s, carry):
            at = pl.ds(aligned(s * BLK, BLK), BLK)
            for c in range(NARROW):
                dst[c, :, at] = src[tab_s[(s // 8) * NARROW + c, lax.rem(s, 8)]]
            return carry

        lax.fori_loop(0, 16, one, 0)

    side = pl.ds(aligned(j * HALF, HALF), HALF)

    def deliver(src, recv, out, first, tall, group):
        wait_bytes(recv.at[pl.ds(0, WIDE - 1)], came.at[src])
        collect(recv, out)
        place = pl.ds(aligned(first, 16), tall)
        for d in range(1, NARROW):
            c = lax.rem(a + d, NARROW)
            remote(out.at[c], modal.at[place, side], group, w, c).start()
        modal[place, side] = out[a]

    deliver(WIDE_A, recv_a, out_a, 48 * h, 16, NARROW_A)
    deliver(WIDE_B, recv_b, out_b, 48 * h + 16, 32, NARROW_B)

    @pl.when(odd == 0)
    def _():
        wait_bytes(recv_l.at[pl.ds(0, WIDE - 1)], came.at[WIDE_L])
        collect(recv_l, out_l)
        for d in range(1, NARROW):
            c = lax.rem(a + d, NARROW)
            remote(out_l.at[c], last.at[j], NARROW_L, w, c).start()
        last[j] = out_l[a]

    wait_bytes(cnt_r.at[pl.ds(0, 3)], came.at[NARROW_C])
    to_scalar = pltpu.make_async_copy(cnt_r, cnt_s, local.at[2])
    to_scalar.start()

    @pl.when(odd == 0)
    def _():
        wait_bytes(last.at[0], came.at[NARROW_L])

    @pl.when(odd == 1)
    def _():
        wait_bytes(last, came.at[NARROW_L])

    to_scalar.wait()
    for p in range(2):
        tiles = last[p].astype(jnp.float32)
        full = tiles[0:8] + tiles[8:16]
        metric[:, p * HALF : (p + 1) * HALF] = full[0:6]
        modal[96:100, p * HALF : (p + 1) * HALF] = jnp.concatenate(
            [tiles[6:8], tiles[14:16]], axis=0
        ).astype(jnp.bfloat16)
        xx, yy, zz = full[0:1], full[1:2], full[2:3]
        xy, xz, yz = full[3:4], full[4:5], full[5:6]
        det = xx * (yy * zz - yz * yz) - xy * (xy * zz - yz * xz) + xz * (xy * yz - yy * xz)
        root = jnp.sqrt(det)
        for s in range(16):
            units = cnt_s[2 * p, (s // 8) * NARROW + a, s % 8].astype(jnp.float32)
            first = p * HALF + s * BLK
            work[:, first : first + BLK] = root[:, s * BLK : (s + 1) * BLK] * units

    wait_bytes(out_a.at[pl.ds(0, 3)], came.at[NARROW_A])
    wait_bytes(out_b.at[pl.ds(0, 3)], came.at[NARROW_B])
    wait_bytes(send_a.at[pl.ds(0, WIDE - 1)], sent.at[WIDE_A])
    wait_bytes(send_b.at[pl.ds(0, WIDE - 1)], sent.at[WIDE_B])
    wait_bytes(tags.at[pl.ds(0, WIDE - 1)], sent.at[WIDE_TAG])
    wait_bytes(cnt_r.at[pl.ds(0, 3)], sent.at[NARROW_C])
    wait_bytes(out_a.at[pl.ds(0, 3)], sent.at[NARROW_A])
    wait_bytes(out_b.at[pl.ds(0, 3)], sent.at[NARROW_B])

    @pl.when(odd == 0)
    def _():
        wait_bytes(send_l.at[pl.ds(0, WIDE // 2 - 1)], sent.at[WIDE_L])
        wait_bytes(out_l.at[pl.ds(0, 3)], sent.at[NARROW_L])

    @pl.when(odd == 1)
    def _():
        wait_bytes(send_l.at[pl.ds(0, WIDE // 2)], sent.at[WIDE_L])


def per_device(coefficients, neighbours, halo_blocks, recon_weight, owner_device, work_count):
    member = lax.axis_index("narrow") % 2
    code = jnp.tile(owner_device + CODE * work_count, 4).reshape(1, BLK)
    lane = lax.broadcasted_iota(jnp.int32, (1, BLK), 1)
    info = jnp.where(lane // BLOCKS == member, code, 0)
    weights = recon_weight.reshape(5, 25, 3, COEF).transpose(3, 0, 2, 1)
    weights = jnp.pad(weights, ((0, 0), (0, 0), (0, 1), (0, 7))).reshape(COEF, 5 * BLK)
    vmem = pl.BlockSpec(memory_space=pltpu.VMEM)
    smem = pl.BlockSpec(memory_space=pltpu.SMEM)
    low, full, whole = jnp.bfloat16, jnp.float32, jnp.int32
    modal, metric, work = pl.pallas_call(
        kernel,
        out_shape=(
            jax.ShapeDtypeStruct((COEF, ELEMS), low),
            jax.ShapeDtypeStruct((6, ELEMS), full),
            jax.ShapeDtypeStruct((1, ELEMS), full),
        ),
        in_specs=[vmem, smem, smem, vmem, vmem],
        out_specs=(vmem, vmem, vmem),
        scratch_shapes=[
            pltpu.VMEM((7, BLOCKS, 16, BLK), low),
            pltpu.VMEM((2 * BLOCKS, 16, BLK), low),
            pltpu.VMEM((2 * BLOCKS, 16, BLK), low),
            pltpu.VMEM((2 * BLOCKS, 16, BLK), low),
            pltpu.VMEM((2 * BLOCKS, 16, BLK), low),
            pltpu.VMEM((1, BLK), whole),
            pltpu.VMEM((1, BLK), whole),
            pltpu.VMEM((8, BLK), whole),
            pltpu.SMEM((8, BLK), whole),
            pltpu.VMEM((8, BLK), whole),
            pltpu.SMEM((8, BLK), whole),
            pltpu.VMEM((8, BLK), whole),
            pltpu.VMEM((NARROW, 8, BLK), whole),
            pltpu.SMEM((NARROW, 8, BLK), whole),
            pltpu.VMEM((4, 2, 7, 16, BLK), low),
            pltpu.VMEM((4, 2, 7, 16, BLK), low),
            pltpu.VMEM((WIDE, 1, BLK), whole),
            pltpu.VMEM((WIDE, BLK), whole),
            pltpu.VMEM((WIDE, 16, BLK), low),
            pltpu.VMEM((WIDE, 16, BLK), low),
            pltpu.VMEM((WIDE, 32, BLK), low),
            pltpu.VMEM((WIDE, 32, BLK), low),
            pltpu.VMEM((WIDE, 16, BLK), low),
            pltpu.VMEM((WIDE, 16, BLK), low),
            pltpu.VMEM((NARROW, 16, HALF), low),
            pltpu.VMEM((NARROW, 32, HALF), low),
            pltpu.VMEM((NARROW, 16, HALF), low),
            pltpu.VMEM((2, 16, HALF), low),
            pltpu.VMEM((4, EXT, BLK), full),
            pltpu.VMEM((ELEMS, BLK), full),
            pltpu.VMEM((ELEMS, BLK), full),
            pltpu.SemaphoreType.DMA((GROUPS,)),
            pltpu.SemaphoreType.DMA((GROUPS,)),
            pltpu.SemaphoreType.DMA((3,)),
        ],
        compiler_params=pltpu.CompilerParams(
            collective_id=0, has_side_effects=True, vmem_limit_bytes=48 * 1024 * 1024
        ),
        name="migrate",
    )(coefficients, neighbours, halo_blocks.reshape(8), weights, info)
    return modal, metric, work.reshape(ELEMS)


def solution(mesh):
    return jax.shard_map(
        per_device,
        mesh=mesh,
        in_specs=(
            P(None, ("wide", "narrow")),
            P(None, ("wide", "narrow")),
            P(("wide", "narrow"), None, None),
            P(),
            P(("wide", "narrow")),
            P(("wide", "narrow")),
        ),
        out_specs=(P(None, ("wide", "narrow")), P(None, ("wide", "narrow")), P(("wide", "narrow"))),
        check_vma=False,
    )
```

```python
import jax
import jax.numpy as jnp
from jax import lax
from jax.experimental import pallas as pl
from jax.experimental.pallas import tpu as pltpu
from jax.sharding import PartitionSpec as P

MESH = pl.DeviceIdType.MESH
WIDE = 128
NARROW = 4
BLK = 128
BLOCKS = 32
ELEMS = BLK * BLOCKS
COEF = 100
HALO = 8 * BLK
EXT = ELEMS + HALO
HALF = 16 * BLK
CODE = 1024

INFO, SWAP_A, SWAP_B, SWAP_C, HALO_UP, HALO_DOWN, HALO_LEFT, HALO_RIGHT = range(8)
WIDE_TAG, WIDE_A, WIDE_B, WIDE_C, SWAP_L, SWAP_M, WIDE_L = range(8, 15)
COUNTS, NARROW_A, NARROW_B, NARROW_C, NARROW_L = range(15, 20)
GROUPS = 20


def aligned(value, step):
    return pl.multiple_of(value, step)


def kernel(
    coef_in, nbr_in, halo, weights, owner, units, modal, last, cnt_r,
    coef, nbr, wts, info,
    tiles, pair_a, pair_b, pair_c, late, pinfo, both, pick_v, pick_s, tab_v, tab_s, cnt_v,
    hsend, hrecv, tags, tags2, send_a, recv_a, send_b, recv_b, send_c, recv_c, send_l, recv_l,
    out_a, out_b, out_c, out_l, table, own, rows, sent, came, local,
):
    w = lax.axis_index("wide")
    a = lax.axis_index("narrow")
    h = lax.rem(a, 2)
    j = a // 2
    partner = a + 1 - 2 * h
    mine = pl.ds(h * BLOCKS, BLOCKS)
    pairs = (pair_a, pair_b, pair_c)

    def remote(src, dst, group, wide, narrow):
        return pltpu.make_async_remote_copy(
            src_ref=src, dst_ref=dst, send_sem=sent.at[group], recv_sem=came.at[group],
            device_id=(wide, narrow), device_id_type=MESH,
        )

    def wait_bytes(ref, sem):
        pltpu.make_async_copy(ref, ref, sem).wait()

    fetch_coef = pltpu.make_async_copy(coef_in, coef, local.at[3])
    fetch_coef.start()
    fetch_nbr = pltpu.make_async_copy(nbr_in, nbr, local.at[4])
    fetch_nbr.start()

    barrier = pltpu.get_barrier_semaphore()

    def greet(i, carry):
        pl.semaphore_signal(barrier, inc=1, device_id=(lax.rem(w + i, WIDE), a), device_id_type=MESH)
        return carry

    for d in range(1, NARROW):
        pl.semaphore_signal(barrier, inc=1, device_id=(w, lax.rem(a + d, NARROW)), device_id_type=MESH)
    lax.fori_loop(1, WIDE, greet, 0)

    lane1 = lax.broadcasted_iota(jnp.int32, (1, BLK), 1)
    code = jnp.zeros((1, BLK), jnp.int32)
    for b in range(BLOCKS):
        code = jnp.where(lane1 == h * BLOCKS + b, owner[b] + CODE * units[b], code)
    info[...] = code
    fetch_coef.wait()

    def retile(b, carry):
        at = pl.ds(aligned(b * BLK, BLK), BLK)
        for k in range(6):
            tiles[k, b] = coef[16 * k : 16 * k + 16, at]
        end = coef[96:100, at]
        tiles[6, b] = jnp.concatenate([end, jnp.zeros((12, BLK), end.dtype)], axis=0)
        return carry

    lax.fori_loop(0, BLOCKS, retile, 0)
    pl.semaphore_wait(barrier, WIDE - 1 + NARROW - 1)

    swap_info = remote(info, pinfo, INFO, w, partner)
    swap_info.start()
    swaps = [
        remote(tiles.at[3 * (1 - h) + k], pairs[k].at[mine], SWAP_A + k, w, partner)
        for k in range(3)
    ]
    swaps[0].start()

    def keep(b, carry):
        for k in range(3):
            pairs[k][h * BLOCKS + b] = tiles[3 * h + k, b]
        return carry

    lax.fori_loop(0, BLOCKS, keep, 0)

    places = [
        (lax.rem(w + WIDE - 1, WIDE), a),
        (lax.rem(w + 1, WIDE), a),
        (w, lax.rem(a + NARROW - 1, NARROW)),
        (w, lax.rem(a + 1, NARROW)),
    ]
    halos = []
    for k in range(4):
        for s in range(2):
            block = halo[0, s, k]
            for r in range(7):
                hsend[k, s, r] = tiles[r, block]
        halos.append(remote(hsend.at[k], hrecv.at[k ^ 1], HALO_UP + k, *places[k]))

    swap_info.wait()
    both[...] = info[...] + pinfo[...]
    entries = jnp.transpose(jnp.broadcast_to(both[...], (BLK, BLK)))
    lane = lax.broadcasted_iota(jnp.int32, (BLK, BLK), 1)
    sub = lax.broadcasted_iota(jnp.int32, (BLK, BLK), 0)
    goes = (entries >= CODE) & ((entries & (CODE - 1)) // NARROW == lane)
    pick = jnp.sum(jnp.where(goes, sub, 0), axis=0, keepdims=True)
    pick_v[...] = jnp.broadcast_to(pick, (8, BLK))
    to_scalar = pltpu.make_async_copy(pick_v, pick_s, local.at[0])
    to_scalar.start()
    to_scalar.wait()

    def spread(src, dst, group):
        def one(i, carry):
            t = lax.rem(w + i, WIDE)
            remote(src.at[t], dst.at[w], group, t, a).start()
            return carry

        lax.fori_loop(1, WIDE, one, 0)

    def send_chunk(pair, src, dst, group):
        def pack(t, carry):
            src[t] = pair[pick_s[0, t]]
            return carry

        lax.fori_loop(0, WIDE, pack, 0)
        dst[w] = src[w]
        spread(src, dst, group)

    swaps[0].wait()
    swaps[1].start()
    swaps[2].start()
    for push in halos:
        push.start()
    send_chunk(pair_a, send_a, recv_a, WIDE_A)
    swaps[1].wait()
    send_chunk(pair_b, send_b, recv_b, WIDE_B)
    def one_tag(i, carry):
        remote(both, tags.at[w], WIDE_TAG, lax.rem(w + i, WIDE), a).start()
        return carry

    tags[w] = both[...]
    lax.fori_loop(1, WIDE, one_tag, 0)

    def product(cols, weights):
        return lax.dot_general(
            cols, weights, (((0,), (0,)), ((), ())), preferred_element_type=jnp.float32
        )

    def own_block(b, carry):
        at = pl.ds(aligned(b * BLK, BLK), BLK)
        result = product(coef[:, at], wts[...])
        own[at, :] = result[:, :BLK]
        for f in range(4):
            table[f, at, :] = result[:, (f + 1) * BLK : (f + 2) * BLK]
        return carry

    place_row = lax.broadcasted_iota(jnp.int32, (75, BLK), 0)
    place_lane = lax.broadcasted_iota(jnp.int32, (75, BLK), 1)
    order = (place_lane % 32 < 25) & (place_row == 3 * (place_lane % 32) + place_lane // 32)
    order = order.astype(jnp.float32).astype(jnp.bfloat16)
    for f in range(5):
        wts[:, f * BLK : (f + 1) * BLK] = product(weights[f], order).astype(jnp.bfloat16)

    lax.fori_loop(0, BLOCKS, own_block, 0)
    for push in halos:
        push.wait()
    for k in range(4):
        for s in range(2):
            result = product(hrecv[k, s].reshape(112, BLK)[:COEF], wts[:, BLK:])
            first = ELEMS + (2 * k + s) * BLK
            for f in range(4):
                table[f, first : first + BLK, :] = result[:, f * BLK : (f + 1) * BLK]

    fetch_nbr.wait()

    def gather(i, carry):
        for u in range(32):
            e = i * 32 + u
            total = table[0, nbr[0, e]]
            for f in range(1, 4):
                total = total + table[f, nbr[f, e]]
            rows[e] = total
        return carry

    lax.fori_loop(0, 64, gather, 0)
    swaps[2].wait()
    send_chunk(pair_c, send_c, recv_c, WIDE_C)

    lax.fori_loop(64, 128, gather, 0)

    def metric_block(b, carry):
        at = pl.ds(aligned(b * BLK, BLK), BLK)
        derivs = jnp.transpose(own[at, :] + rows[at, :])
        x, y, z = derivs[0:32], derivs[32:64], derivs[64:96]

        def mean(left, right, base):
            return base + jnp.sum(left * right, axis=0, keepdims=True) * (1.0 / 25)

        full = jnp.concatenate(
            [mean(x, x, 1.0), mean(y, y, 1.0), mean(z, z, 1.0), mean(x, y, 0.0), mean(x, z, 0.0), mean(y, z, 0.0)],
            axis=0,
        )
        high = full.astype(jnp.bfloat16).astype(jnp.float32)
        tail = coef[96:100, at].astype(jnp.float32)
        tile = jnp.concatenate([high, tail[0:2], full - high, tail[2:4]], axis=0)
        late[h * BLOCKS + b] = tile.astype(jnp.bfloat16)
        return carry

    late_swaps = []
    for part in range(2):
        count_half = BLOCKS // 2
        lax.fori_loop(part * count_half, (part + 1) * count_half, metric_block, 0)
        half = late.at[pl.ds(h * BLOCKS + part * count_half, count_half)]
        late_swaps.append(remote(half, half, SWAP_L + part, w, partner))
        late_swaps[-1].start()
    for swap in late_swaps:
        swap.wait()
    odd = lax.rem(w + h, 2)

    def pack_l(i, carry):
        t = 2 * i + h
        send_l[t] = late[pick_s[0, t]]
        return carry

    lax.fori_loop(0, WIDE // 2, pack_l, 0)

    def send_late(i, carry):
        t = lax.rem(w + 2 * i + odd, WIDE)
        remote(send_l.at[t], recv_l.at[w], WIDE_L, t, a).start()
        return carry

    @pl.when(odd == 0)
    def _():
        recv_l[w] = send_l[w]

    lax.fori_loop(1 - odd, WIDE // 2, send_late, 0)

    wait_bytes(tags.at[pl.ds(0, WIDE - 1)], came.at[WIDE_TAG])

    def flat(i, carry):
        tags2[pl.ds(i, 1), :] = tags[i]
        return carry

    lax.fori_loop(0, WIDE, flat, 0)
    codes = jnp.transpose(tags2[...])
    here = (codes >= CODE) & ((codes & (CODE - 1)) // NARROW == w)
    kinds = jnp.where(here, (sub // BLOCKS) * NARROW + lax.rem(codes, NARROW) + 1, 0)
    kind = jnp.sum(kinds, axis=0, keepdims=True) - 1
    count = jnp.sum(jnp.where(here, codes // CODE, 0), axis=0, keepdims=True)
    lane8 = lax.broadcasted_iota(jnp.int32, (8, BLK), 1)
    sub8 = lax.broadcasted_iota(jnp.int32, (8, BLK), 0)
    chosen = (jnp.broadcast_to(kind, (8, BLK)) == sub8).astype(jnp.int32)
    rank = chosen
    for step in (1, 2, 4, 8, 16, 32, 64):
        rank = rank + jnp.where(lane8 >= step, pltpu.roll(rank, step, 1), 0)
    rank = rank - chosen
    counts = jnp.broadcast_to(count, (8, BLK))
    froms = jnp.zeros((8, BLK), jnp.int32)
    works = jnp.zeros((8, BLK), jnp.int32)
    for r in range(8):
        found = (chosen > 0) & (rank == r)
        froms = jnp.where(
            lane8 == r, jnp.sum(jnp.where(found, lane8, 0), axis=1, keepdims=True), froms
        )
        works = jnp.where(
            lane8 == r, jnp.sum(jnp.where(found, counts, 0), axis=1, keepdims=True), works
        )
    tab_v[...] = froms
    cnt_v[...] = works
    to_scalar = pltpu.make_async_copy(tab_v, tab_s, local.at[1])
    to_scalar.start()
    to_scalar.wait()
    cnt_r[a] = cnt_v[...]
    for d in range(1, NARROW):
        remote(cnt_v, cnt_r.at[a], COUNTS, w, lax.rem(a + d, NARROW)).start()

    def collect(src, dst):
        def one(s, carry):
            at = pl.ds(aligned(s * BLK, BLK), BLK)
            for c in range(NARROW):
                dst[c, :, at] = src[tab_s[(s // 8) * NARROW + c, lax.rem(s, 8)]]
            return carry

        lax.fori_loop(0, 16, one, 0)

    side = pl.ds(aligned(j * HALF, HALF), HALF)

    def deliver(src, recv, out, first, group):
        wait_bytes(recv.at[pl.ds(0, WIDE - 1)], came.at[src])
        collect(recv, out)
        place = pl.ds(aligned(first, 16), 16)
        for d in range(1, NARROW):
            c = lax.rem(a + d, NARROW)
            remote(out.at[c], modal.at[place, side], group, w, c).start()
        modal[place, side] = out[a]

    deliver(WIDE_A, recv_a, out_a, 48 * h, NARROW_A)
    deliver(WIDE_B, recv_b, out_b, 48 * h + 16, NARROW_B)
    deliver(WIDE_C, recv_c, out_c, 48 * h + 32, NARROW_C)

    @pl.when(odd == 0)
    def _():
        wait_bytes(recv_l.at[pl.ds(0, WIDE - 1)], came.at[WIDE_L])
        collect(recv_l, out_l)
        for d in range(1, NARROW):
            c = lax.rem(a + d, NARROW)
            remote(out_l.at[c], last.at[j], NARROW_L, w, c).start()
        last[j] = out_l[a]

    wait_bytes(cnt_r.at[pl.ds(0, 3)], came.at[COUNTS])

    @pl.when(odd == 0)
    def _():
        wait_bytes(last.at[0], came.at[NARROW_L])

    @pl.when(odd == 1)
    def _():
        wait_bytes(last, came.at[NARROW_L])

    wait_bytes(out_a.at[pl.ds(0, 3)], came.at[NARROW_A])
    wait_bytes(out_b.at[pl.ds(0, 3)], came.at[NARROW_B])
    wait_bytes(send_a.at[pl.ds(0, WIDE - 1)], sent.at[WIDE_A])
    wait_bytes(send_b.at[pl.ds(0, WIDE - 1)], sent.at[WIDE_B])
    wait_bytes(tags.at[pl.ds(0, WIDE - 1)], sent.at[WIDE_TAG])
    wait_bytes(cnt_r.at[pl.ds(0, 3)], sent.at[COUNTS])
    wait_bytes(send_c.at[pl.ds(0, WIDE - 1)], sent.at[WIDE_C])
    wait_bytes(out_c.at[pl.ds(0, 3)], came.at[NARROW_C])
    wait_bytes(out_c.at[pl.ds(0, 3)], sent.at[NARROW_C])
    wait_bytes(out_a.at[pl.ds(0, 3)], sent.at[NARROW_A])
    wait_bytes(out_b.at[pl.ds(0, 3)], sent.at[NARROW_B])

    @pl.when(odd == 0)
    def _():
        wait_bytes(send_l.at[pl.ds(0, WIDE // 2 - 1)], sent.at[WIDE_L])
        wait_bytes(out_l.at[pl.ds(0, 3)], sent.at[NARROW_L])

    @pl.when(odd == 1)
    def _():
        wait_bytes(send_l.at[pl.ds(0, WIDE // 2)], sent.at[WIDE_L])


def finish(moved, last, counts, modal, metric, work):
    p = pl.program_id(0)
    a = lax.axis_index("narrow")
    modal[0:96] = moved[...]
    tiles = last[0].astype(jnp.float32)
    full = tiles[0:8] + tiles[8:16]
    metric[...] = full[0:6]
    modal[96:100] = jnp.concatenate([tiles[6:8], tiles[14:16]], axis=0).astype(jnp.bfloat16)
    xx, yy, zz = full[0:1], full[1:2], full[2:3]
    xy, xz, yz = full[3:4], full[4:5], full[5:6]
    det = xx * (yy * zz - yz * yz) - xy * (xy * zz - yz * xz) + xz * (xy * yz - yy * xz)
    root = jnp.sqrt(det)
    for s in range(16):
        units = counts[2 * p, (s // 8) * NARROW + a, s % 8].astype(jnp.float32)
        work[:, s * BLK : (s + 1) * BLK] = root[:, s * BLK : (s + 1) * BLK] * units


def per_device(coefficients, neighbours, halo_blocks, recon_weight, owner_device, work_count):
    vmem = pl.BlockSpec(memory_space=pltpu.VMEM)
    smem = pl.BlockSpec(memory_space=pltpu.SMEM)
    hbm = pl.BlockSpec(memory_space=pl.ANY)
    low, full, whole = jnp.bfloat16, jnp.float32, jnp.int32
    moved, last, counts = pl.pallas_call(
        kernel,
        out_shape=(
            jax.ShapeDtypeStruct((96, ELEMS), low),
            jax.ShapeDtypeStruct((2, 16, HALF), low),
            jax.ShapeDtypeStruct((NARROW, 8, BLK), whole),
        ),
        in_specs=[hbm, hbm, smem, vmem, smem, smem],
        out_specs=(vmem, vmem, vmem),
        scratch_shapes=[
            pltpu.VMEM((COEF, ELEMS), low),
            pltpu.SMEM((4, ELEMS), whole),
            pltpu.VMEM((COEF, 5 * BLK), low),
            pltpu.VMEM((1, BLK), whole),
            pltpu.VMEM((7, BLOCKS, 16, BLK), low),
            pltpu.VMEM((2 * BLOCKS, 16, BLK), low),
            pltpu.VMEM((2 * BLOCKS, 16, BLK), low),
            pltpu.VMEM((2 * BLOCKS, 16, BLK), low),
            pltpu.VMEM((2 * BLOCKS, 16, BLK), low),
            pltpu.VMEM((1, BLK), whole),
            pltpu.VMEM((1, BLK), whole),
            pltpu.VMEM((8, BLK), whole),
            pltpu.SMEM((8, BLK), whole),
            pltpu.VMEM((8, BLK), whole),
            pltpu.SMEM((8, BLK), whole),
            pltpu.VMEM((8, BLK), whole),
            pltpu.VMEM((4, 2, 7, 16, BLK), low),
            pltpu.VMEM((4, 2, 7, 16, BLK), low),
            pltpu.VMEM((WIDE, 1, BLK), whole),
            pltpu.VMEM((WIDE, BLK), whole),
            pltpu.VMEM((WIDE, 16, BLK), low),
            pltpu.VMEM((WIDE, 16, BLK), low),
            pltpu.VMEM((WIDE, 16, BLK), low),
            pltpu.VMEM((WIDE, 16, BLK), low),
            pltpu.VMEM((WIDE, 16, BLK), low),
            pltpu.VMEM((WIDE, 16, BLK), low),
            pltpu.VMEM((WIDE, 16, BLK), low),
            pltpu.VMEM((WIDE, 16, BLK), low),
            pltpu.VMEM((NARROW, 16, HALF), low),
            pltpu.VMEM((NARROW, 16, HALF), low),
            pltpu.VMEM((NARROW, 16, HALF), low),
            pltpu.VMEM((NARROW, 16, HALF), low),
            pltpu.VMEM((4, EXT, BLK), full),
            pltpu.VMEM((ELEMS, BLK), full),
            pltpu.VMEM((ELEMS, BLK), full),
            pltpu.SemaphoreType.DMA((GROUPS,)),
            pltpu.SemaphoreType.DMA((GROUPS,)),
            pltpu.SemaphoreType.DMA((5,)),
        ],
        compiler_params=pltpu.CompilerParams(
            collective_id=0, has_side_effects=True, vmem_limit_bytes=63 * 1024 * 1024
        ),
        name="migrate",
    )(coefficients, neighbours, halo_blocks.transpose(0, 2, 1), recon_weight, owner_device, work_count)
    modal, metric, work = pl.pallas_call(
        finish,
        grid=(2,),
        out_shape=(
            jax.ShapeDtypeStruct((COEF, ELEMS), low),
            jax.ShapeDtypeStruct((6, ELEMS), full),
            jax.ShapeDtypeStruct((1, ELEMS), full),
        ),
        in_specs=[
            pl.BlockSpec((96, HALF), lambda p: (0, p)),
            pl.BlockSpec((1, 16, HALF), lambda p: (p, 0, 0)),
            smem,
        ],
        out_specs=(
            pl.BlockSpec((COEF, HALF), lambda p: (0, p)),
            pl.BlockSpec((6, HALF), lambda p: (0, p)),
            pl.BlockSpec((1, HALF), lambda p: (0, p)),
        ),
        name="finish",
    )(moved, last, counts)
    return modal, metric, work.reshape(ELEMS)


def solution(mesh):
    return jax.shard_map(
        per_device,
        mesh=mesh,
        in_specs=(
            P(None, ("wide", "narrow")),
            P(None, ("wide", "narrow")),
            P(("wide", "narrow"), None, None),
            P(),
            P(("wide", "narrow")),
            P(("wide", "narrow")),
        ),
        out_specs=(P(None, ("wide", "narrow")), P(None, ("wide", "narrow")), P(("wide", "narrow"))),
        check_vma=False,
    )
```

```python
import jax
import jax.numpy as jnp
from jax import lax
from jax.experimental import pallas as pl
from jax.experimental.pallas import tpu as pltpu
from jax.sharding import PartitionSpec as P

MESH = pl.DeviceIdType.MESH
WIDE = 128
NARROW = 4
BLK = 128
BLOCKS = 32
ELEMS = BLK * BLOCKS
COEF = 100
HALO = 8 * BLK
EXT = ELEMS + HALO
HALF = 16 * BLK
CODE = 1024

INFO, SWAP_A, SWAP_B, SWAP_C, HALO_UP, HALO_DOWN, HALO_LEFT, HALO_RIGHT = range(8)
WIDE_TAG, WIDE_A, WIDE_B, WIDE_C, SWAP_L, SWAP_M, WIDE_L = range(8, 15)
COUNTS, NARROW_A, NARROW_B, NARROW_C, NARROW_L = range(15, 20)
GROUPS = 20


def aligned(value, step):
    return pl.multiple_of(value, step)


def eights(step):
    def some(i, carry):
        for u in range(8):
            carry = step(8 * i + u, carry)
        return carry

    return some


def sevens(step):
    def some(i, carry):
        for u in range(7):
            carry = step(7 * i + u + 1, carry)
        return carry

    return some


def kernel(
    coef_in, nbr_in, halo, weights, owner, units, modal, last, cnt_r,
    coef, nbr, wts, info,
    tiles, pair_a, pair_b, pair_c, late, pinfo, both, pick_v, pick_s, tab_v, tab_s, cnt_v,
    hsend, hrecv, tags, tags2, send_a, recv_a, send_b, recv_b, send_c, recv_c, send_l, recv_l,
    out_a, out_b, out_c, out_l, table, own, rows, sent, came, local,
):
    w = lax.axis_index("wide")
    a = lax.axis_index("narrow")
    h = lax.rem(a, 2)
    j = a // 2
    partner = a + 1 - 2 * h
    mine = pl.ds(h * BLOCKS, BLOCKS)
    pairs = (pair_a, pair_b, pair_c)

    def remote(src, dst, group, wide, narrow):
        return pltpu.make_async_remote_copy(
            src_ref=src, dst_ref=dst, send_sem=sent.at[group], recv_sem=came.at[group],
            device_id=(wide, narrow), device_id_type=MESH,
        )

    def wait_bytes(ref, sem):
        pltpu.make_async_copy(ref, ref, sem).wait()

    fetch_coef = pltpu.make_async_copy(coef_in, coef, local.at[3])
    fetch_coef.start()
    fetch_nbr = pltpu.make_async_copy(nbr_in, nbr, local.at[4])
    fetch_nbr.start()

    barrier = pltpu.get_barrier_semaphore()

    def greet(i, carry):
        pl.semaphore_signal(barrier, inc=1, device_id=(lax.rem(w + i, WIDE), a), device_id_type=MESH)
        return carry

    for d in range(1, NARROW):
        pl.semaphore_signal(barrier, inc=1, device_id=(w, lax.rem(a + d, NARROW)), device_id_type=MESH)
    lax.fori_loop(0, 18, sevens(greet), 0)
    greet(WIDE - 1, 0)

    lane1 = lax.broadcasted_iota(jnp.int32, (1, BLK), 1)
    code = jnp.zeros((1, BLK), jnp.int32)
    for b in range(BLOCKS):
        code = jnp.where(lane1 == h * BLOCKS + b, owner[b] + CODE * units[b], code)
    info[...] = code
    fetch_coef.wait()

    def retile(b, carry):
        at = pl.ds(aligned(b * BLK, BLK), BLK)
        for k in range(6):
            tiles[k, b] = coef[16 * k : 16 * k + 16, at]
        end = coef[96:100, at]
        tiles[6, b] = jnp.concatenate([end, jnp.zeros((12, BLK), end.dtype)], axis=0)
        return carry

    lax.fori_loop(0, BLOCKS, retile, 0)
    pl.semaphore_wait(barrier, WIDE - 1 + NARROW - 1)

    swap_info = remote(info, pinfo, INFO, w, partner)
    swap_info.start()
    swaps = [
        remote(tiles.at[3 * (1 - h) + k], pairs[k].at[mine], SWAP_A + k, w, partner)
        for k in range(3)
    ]
    swaps[0].start()

    def keep(b, carry):
        for k in range(3):
            pairs[k][h * BLOCKS + b] = tiles[3 * h + k, b]
        return carry

    lax.fori_loop(0, BLOCKS, keep, 0)

    places = [
        (lax.rem(w + WIDE - 1, WIDE), a),
        (lax.rem(w + 1, WIDE), a),
        (w, lax.rem(a + NARROW - 1, NARROW)),
        (w, lax.rem(a + 1, NARROW)),
    ]
    halos = []
    for k in range(4):
        for s in range(2):
            block = halo[0, s, k]
            for r in range(7):
                hsend[k, s, r] = tiles[r, block]
        halos.append(remote(hsend.at[k], hrecv.at[k ^ 1], HALO_UP + k, *places[k]))

    swap_info.wait()
    both[...] = info[...] + pinfo[...]
    entries = jnp.transpose(jnp.broadcast_to(both[...], (BLK, BLK)))
    lane = lax.broadcasted_iota(jnp.int32, (BLK, BLK), 1)
    sub = lax.broadcasted_iota(jnp.int32, (BLK, BLK), 0)
    goes = (entries >= CODE) & ((entries & (CODE - 1)) // NARROW == lane)
    pick = jnp.sum(jnp.where(goes, sub, 0), axis=0, keepdims=True)
    pick_v[...] = jnp.broadcast_to(pick, (8, BLK))
    to_scalar = pltpu.make_async_copy(pick_v, pick_s, local.at[0])
    to_scalar.start()
    to_scalar.wait()

    def spread(src, dst, group):
        def one(i, carry):
            t = lax.rem(w + i, WIDE)
            remote(src.at[t], dst.at[w], group, t, a).start()
            return carry

        lax.fori_loop(0, 18, sevens(one), 0)
        one(WIDE - 1, 0)

    def send_chunk(pair, src, dst, group):
        def pack(t, carry):
            src[t] = pair[pick_s[0, t]]
            return carry

        lax.fori_loop(0, WIDE // 8, eights(pack), 0)
        dst[w] = src[w]
        spread(src, dst, group)

    swaps[0].wait()
    swaps[1].start()
    swaps[2].start()
    for push in halos:
        push.start()
    send_chunk(pair_a, send_a, recv_a, WIDE_A)
    swaps[1].wait()
    send_chunk(pair_b, send_b, recv_b, WIDE_B)
    def one_tag(i, carry):
        remote(both, tags.at[w], WIDE_TAG, lax.rem(w + i, WIDE), a).start()
        return carry

    tags[w] = both[...]
    lax.fori_loop(1, WIDE, one_tag, 0)

    def product(cols, weights):
        return lax.dot_general(
            cols, weights, (((0,), (0,)), ((), ())), preferred_element_type=jnp.float32
        )

    def own_block(b, carry):
        at = pl.ds(aligned(b * BLK, BLK), BLK)
        result = product(coef[:, at], wts[...])
        own[at, :] = result[:, :BLK]
        for f in range(4):
            table[f, at, :] = result[:, (f + 1) * BLK : (f + 2) * BLK]
        return carry

    place_row = lax.broadcasted_iota(jnp.int32, (75, BLK), 0)
    place_lane = lax.broadcasted_iota(jnp.int32, (75, BLK), 1)
    order = (place_lane % 32 < 25) & (place_row == 3 * (place_lane % 32) + place_lane // 32)
    order = order.astype(jnp.float32).astype(jnp.bfloat16)
    for f in range(5):
        wts[:, f * BLK : (f + 1) * BLK] = product(weights[f], order).astype(jnp.bfloat16)

    lax.fori_loop(0, BLOCKS, own_block, 0)
    for push in halos:
        push.wait()
    for k in range(4):
        for s in range(2):
            result = product(hrecv[k, s].reshape(112, BLK)[:COEF], wts[:, BLK:])
            first = ELEMS + (2 * k + s) * BLK
            for f in range(4):
                table[f, first : first + BLK, :] = result[:, f * BLK : (f + 1) * BLK]

    fetch_nbr.wait()

    def gather(i, carry):
        for group in range(4):
            totals = []
            for u in range(8):
                e = i * 32 + group * 8 + u
                total = table[0, nbr[0, e]]
                for f in range(1, 4):
                    total = total + table[f, nbr[f, e]]
                totals.append(total)
            for u in range(8):
                rows[i * 32 + group * 8 + u] = totals[u]
        return carry

    lax.fori_loop(0, 64, gather, 0)
    swaps[2].wait()
    send_chunk(pair_c, send_c, recv_c, WIDE_C)

    lax.fori_loop(64, 128, gather, 0)

    def metric_block(b, carry):
        at = pl.ds(aligned(b * BLK, BLK), BLK)
        derivs = jnp.transpose(own[at, :] + rows[at, :])
        x, y, z = derivs[0:32], derivs[32:64], derivs[64:96]

        def mean(left, right, base):
            return base + jnp.sum(left * right, axis=0, keepdims=True) * (1.0 / 25)

        full = jnp.concatenate(
            [mean(x, x, 1.0), mean(y, y, 1.0), mean(z, z, 1.0), mean(x, y, 0.0), mean(x, z, 0.0), mean(y, z, 0.0)],
            axis=0,
        )
        high = full.astype(jnp.bfloat16).astype(jnp.float32)
        tail = coef[96:100, at].astype(jnp.float32)
        tile = jnp.concatenate([high, tail[0:2], full - high, tail[2:4]], axis=0)
        late[h * BLOCKS + b] = tile.astype(jnp.bfloat16)
        return carry

    late_swaps = []
    for part in range(2):
        count_half = BLOCKS // 2
        lax.fori_loop(part * count_half, (part + 1) * count_half, metric_block, 0)
        half = late.at[pl.ds(h * BLOCKS + part * count_half, count_half)]
        late_swaps.append(remote(half, half, SWAP_L + part, w, partner))
        late_swaps[-1].start()
    for swap in late_swaps:
        swap.wait()
    odd = lax.rem(w + h, 2)

    def pack_l(i, carry):
        t = 2 * i + h
        send_l[t] = late[pick_s[0, t]]
        return carry

    lax.fori_loop(0, WIDE // 16, eights(pack_l), 0)

    def send_late(i, carry):
        t = lax.rem(w + 2 * i + odd, WIDE)
        remote(send_l.at[t], recv_l.at[w], WIDE_L, t, a).start()
        return carry

    @pl.when(odd == 0)
    def _():
        recv_l[w] = send_l[w]

    lax.fori_loop(1 - odd, WIDE // 2, send_late, 0)

    wait_bytes(tags.at[pl.ds(0, WIDE - 1)], came.at[WIDE_TAG])

    def flat(i, carry):
        tags2[pl.ds(i, 1), :] = tags[i]
        return carry

    lax.fori_loop(0, WIDE // 8, eights(flat), 0)
    codes = jnp.transpose(tags2[...])
    here = (codes >= CODE) & ((codes & (CODE - 1)) // NARROW == w)
    kinds = jnp.where(here, (sub // BLOCKS) * NARROW + lax.rem(codes, NARROW) + 1, 0)
    kind = jnp.sum(kinds, axis=0, keepdims=True) - 1
    count = jnp.sum(jnp.where(here, codes // CODE, 0), axis=0, keepdims=True)
    lane8 = lax.broadcasted_iota(jnp.int32, (8, BLK), 1)
    sub8 = lax.broadcasted_iota(jnp.int32, (8, BLK), 0)
    chosen = (jnp.broadcast_to(kind, (8, BLK)) == sub8).astype(jnp.int32)
    rank = chosen
    for step in (1, 2, 4, 8, 16, 32, 64):
        rank = rank + jnp.where(lane8 >= step, pltpu.roll(rank, step, 1), 0)
    rank = rank - chosen
    counts = jnp.broadcast_to(count, (8, BLK))
    froms = jnp.zeros((8, BLK), jnp.int32)
    works = jnp.zeros((8, BLK), jnp.int32)
    for r in range(8):
        found = (chosen > 0) & (rank == r)
        froms = jnp.where(
            lane8 == r, jnp.sum(jnp.where(found, lane8, 0), axis=1, keepdims=True), froms
        )
        works = jnp.where(
            lane8 == r, jnp.sum(jnp.where(found, counts, 0), axis=1, keepdims=True), works
        )
    tab_v[...] = froms
    cnt_v[...] = works
    to_scalar = pltpu.make_async_copy(tab_v, tab_s, local.at[1])
    to_scalar.start()
    to_scalar.wait()
    cnt_r[a] = cnt_v[...]
    for d in range(1, NARROW):
        remote(cnt_v, cnt_r.at[a], COUNTS, w, lax.rem(a + d, NARROW)).start()

    def collect(src, dst):
        def one(s, carry):
            at = pl.ds(aligned(s * BLK, BLK), BLK)
            for c in range(NARROW):
                dst[c, :, at] = src[tab_s[(s // 8) * NARROW + c, lax.rem(s, 8)]]
            return carry

        lax.fori_loop(0, 2, eights(one), 0)

    side = pl.ds(aligned(j * HALF, HALF), HALF)

    def deliver(src, recv, out, first, group):
        wait_bytes(recv.at[pl.ds(0, WIDE - 1)], came.at[src])
        collect(recv, out)
        place = pl.ds(aligned(first, 16), 16)
        for d in range(1, NARROW):
            c = lax.rem(a + d, NARROW)
            remote(out.at[c], modal.at[place, side], group, w, c).start()
        modal[place, side] = out[a]

    deliver(WIDE_A, recv_a, out_a, 48 * h, NARROW_A)
    deliver(WIDE_B, recv_b, out_b, 48 * h + 16, NARROW_B)
    deliver(WIDE_C, recv_c, out_c, 48 * h + 32, NARROW_C)

    @pl.when(odd == 0)
    def _():
        wait_bytes(recv_l.at[pl.ds(0, WIDE - 1)], came.at[WIDE_L])
        collect(recv_l, out_l)
        for d in range(1, NARROW):
            c = lax.rem(a + d, NARROW)
            remote(out_l.at[c], last.at[j], NARROW_L, w, c).start()
        last[j] = out_l[a]

    wait_bytes(cnt_r.at[pl.ds(0, 3)], came.at[COUNTS])

    @pl.when(odd == 0)
    def _():
        wait_bytes(last.at[0], came.at[NARROW_L])

    @pl.when(odd == 1)
    def _():
        wait_bytes(last, came.at[NARROW_L])

    wait_bytes(out_a.at[pl.ds(0, 3)], came.at[NARROW_A])
    wait_bytes(out_b.at[pl.ds(0, 3)], came.at[NARROW_B])
    wait_bytes(send_a.at[pl.ds(0, WIDE - 1)], sent.at[WIDE_A])
    wait_bytes(send_b.at[pl.ds(0, WIDE - 1)], sent.at[WIDE_B])
    wait_bytes(tags.at[pl.ds(0, WIDE - 1)], sent.at[WIDE_TAG])
    wait_bytes(cnt_r.at[pl.ds(0, 3)], sent.at[COUNTS])
    wait_bytes(send_c.at[pl.ds(0, WIDE - 1)], sent.at[WIDE_C])
    wait_bytes(out_c.at[pl.ds(0, 3)], came.at[NARROW_C])
    wait_bytes(out_c.at[pl.ds(0, 3)], sent.at[NARROW_C])
    wait_bytes(out_a.at[pl.ds(0, 3)], sent.at[NARROW_A])
    wait_bytes(out_b.at[pl.ds(0, 3)], sent.at[NARROW_B])

    @pl.when(odd == 0)
    def _():
        wait_bytes(send_l.at[pl.ds(0, WIDE // 2 - 1)], sent.at[WIDE_L])
        wait_bytes(out_l.at[pl.ds(0, 3)], sent.at[NARROW_L])

    @pl.when(odd == 1)
    def _():
        wait_bytes(send_l.at[pl.ds(0, WIDE // 2)], sent.at[WIDE_L])


def finish(moved, last, counts, modal, metric, work):
    p = pl.program_id(0)
    a = lax.axis_index("narrow")
    modal[0:96] = moved[...]
    tiles = last[0].astype(jnp.float32)
    full = tiles[0:8] + tiles[8:16]
    metric[...] = full[0:6]
    modal[96:100] = jnp.concatenate([tiles[6:8], tiles[14:16]], axis=0).astype(jnp.bfloat16)
    xx, yy, zz = full[0:1], full[1:2], full[2:3]
    xy, xz, yz = full[3:4], full[4:5], full[5:6]
    det = xx * (yy * zz - yz * yz) - xy * (xy * zz - yz * xz) + xz * (xy * yz - yy * xz)
    root = jnp.sqrt(det)
    for s in range(16):
        units = counts[2 * p, (s // 8) * NARROW + a, s % 8].astype(jnp.float32)
        work[:, s * BLK : (s + 1) * BLK] = root[:, s * BLK : (s + 1) * BLK] * units


def per_device(coefficients, neighbours, halo_blocks, recon_weight, owner_device, work_count):
    vmem = pl.BlockSpec(memory_space=pltpu.VMEM)
    smem = pl.BlockSpec(memory_space=pltpu.SMEM)
    hbm = pl.BlockSpec(memory_space=pl.ANY)
    low, full, whole = jnp.bfloat16, jnp.float32, jnp.int32
    moved, last, counts = pl.pallas_call(
        kernel,
        out_shape=(
            jax.ShapeDtypeStruct((96, ELEMS), low),
            jax.ShapeDtypeStruct((2, 16, HALF), low),
            jax.ShapeDtypeStruct((NARROW, 8, BLK), whole),
        ),
        in_specs=[hbm, hbm, smem, vmem, smem, smem],
        out_specs=(vmem, vmem, vmem),
        scratch_shapes=[
            pltpu.VMEM((COEF, ELEMS), low),
            pltpu.SMEM((4, ELEMS), whole),
            pltpu.VMEM((COEF, 5 * BLK), low),
            pltpu.VMEM((1, BLK), whole),
            pltpu.VMEM((7, BLOCKS, 16, BLK), low),
            pltpu.VMEM((2 * BLOCKS, 16, BLK), low),
            pltpu.VMEM((2 * BLOCKS, 16, BLK), low),
            pltpu.VMEM((2 * BLOCKS, 16, BLK), low),
            pltpu.VMEM((2 * BLOCKS, 16, BLK), low),
            pltpu.VMEM((1, BLK), whole),
            pltpu.VMEM((1, BLK), whole),
            pltpu.VMEM((8, BLK), whole),
            pltpu.SMEM((8, BLK), whole),
            pltpu.VMEM((8, BLK), whole),
            pltpu.SMEM((8, BLK), whole),
            pltpu.VMEM((8, BLK), whole),
            pltpu.VMEM((4, 2, 7, 16, BLK), low),
            pltpu.VMEM((4, 2, 7, 16, BLK), low),
            pltpu.VMEM((WIDE, 1, BLK), whole),
            pltpu.VMEM((WIDE, BLK), whole),
            pltpu.VMEM((WIDE, 16, BLK), low),
            pltpu.VMEM((WIDE, 16, BLK), low),
            pltpu.VMEM((WIDE, 16, BLK), low),
            pltpu.VMEM((WIDE, 16, BLK), low),
            pltpu.VMEM((WIDE, 16, BLK), low),
            pltpu.VMEM((WIDE, 16, BLK), low),
            pltpu.VMEM((WIDE, 16, BLK), low),
            pltpu.VMEM((WIDE, 16, BLK), low),
            pltpu.VMEM((NARROW, 16, HALF), low),
            pltpu.VMEM((NARROW, 16, HALF), low),
            pltpu.VMEM((NARROW, 16, HALF), low),
            pltpu.VMEM((NARROW, 16, HALF), low),
            pltpu.VMEM((4, EXT, BLK), full),
            pltpu.VMEM((ELEMS, BLK), full),
            pltpu.VMEM((ELEMS, BLK), full),
            pltpu.SemaphoreType.DMA((GROUPS,)),
            pltpu.SemaphoreType.DMA((GROUPS,)),
            pltpu.SemaphoreType.DMA((5,)),
        ],
        compiler_params=pltpu.CompilerParams(
            collective_id=0, has_side_effects=True, vmem_limit_bytes=63 * 1024 * 1024
        ),
        name="migrate",
    )(coefficients, neighbours, halo_blocks.transpose(0, 2, 1), recon_weight, owner_device, work_count)
    modal, metric, work = pl.pallas_call(
        finish,
        grid=(2,),
        out_shape=(
            jax.ShapeDtypeStruct((COEF, ELEMS), low),
            jax.ShapeDtypeStruct((6, ELEMS), full),
            jax.ShapeDtypeStruct((1, ELEMS), full),
        ),
        in_specs=[
            pl.BlockSpec((96, HALF), lambda p: (0, p)),
            pl.BlockSpec((1, 16, HALF), lambda p: (p, 0, 0)),
            smem,
        ],
        out_specs=(
            pl.BlockSpec((COEF, HALF), lambda p: (0, p)),
            pl.BlockSpec((6, HALF), lambda p: (0, p)),
            pl.BlockSpec((1, HALF), lambda p: (0, p)),
        ),
        name="finish",
    )(moved, last, counts)
    return modal, metric, work.reshape(ELEMS)


def solution(mesh):
    return jax.shard_map(
        per_device,
        mesh=mesh,
        in_specs=(
            P(None, ("wide", "narrow")),
            P(None, ("wide", "narrow")),
            P(("wide", "narrow"), None, None),
            P(),
            P(("wide", "narrow")),
            P(("wide", "narrow")),
        ),
        out_specs=(P(None, ("wide", "narrow")), P(None, ("wide", "narrow")), P(("wide", "narrow"))),
        check_vma=False,
    )
```
